512 devices in a mesh: section: 4 (over x), tensor: 16 (over z, y_lo), seq: 8 (over y_hi, core).
Axes of the slice: x: 4, y: 8 (y_hi: 4, y_lo: 2; y = y_hi * 2 + y_lo), z: 8, core: 2. Of those that a mesh axis runs over, the one named last changes fastest.
Arguments:
- stream: bfloat16 [4, 768, 6144], P('section', 'tensor', 'seq'), may hold values from -6 to 6
- norm_gain: float32 [4, 6144], P('section', 'seq'), may hold values from 0.5 to 1.5
- qkv_weight: bfloat16 [4, 6144, 3, 4096], P('section', 'seq', None, 'tensor'), may hold values from -0.078125 to 0.078125
- up_weight: bfloat16 [4, 6144, 12288], P('section', 'seq', 'tensor'), may hold values from -0.078125 to 0.078125
- out_weight: bfloat16 [4, 4096, 6144], P('section', 'tensor', 'seq'), may hold values from -0.375 to 0.375
- down_weight: bfloat16 [4, 12288, 6144], P('section', 'tensor', 'seq'), may hold values from -0.0546875 to 0.0546875
- slot_bias: float32 [4, 32, 27], P('section', 'tensor'), may hold values from -3 to 300
- neighbours: int32 [4, 24, 27], P('section', 'seq'), may hold values from 0 to 23, as said below
- present: int32 [4, 24, 27], P('section', 'seq'), may hold values from 0 to 1, as said below
- brick_slot: int32 [4, 24], P('section'), may hold values from 0 to 23, as said below
Outputs:
- stream_next: bfloat16 [4, 768, 6144], P('section', 'tensor', 'seq')
The draws below stay inside these ranges and needn't reach their ends.
Inputs may be any that keep to these rules, and one draw needn't show every extreme that they name: `neighbours`: entry j of row r names the brick at offset j from the brick held in slot r (offsets -1, 0, 1 along each of three dimensions, the first slowest) when that place is occupied; otherwise its flag in present is 0 and it names the brick itself. Entry 13 is the brick itself. Flagged entries of a row are distinct. `present`: entry 13 of every row is 1. `brick_slot`: each section's row is a permutation of the 24 bricks.
All inputs are finite; a program needn't handle non-finite values.
Results may differ from the reference program's by a relative error of at most 0.025.
Values may be sent and summed in bfloat16 or wider, within the bound.
A program may use at most 64 MiB of HBM per device.

```python
import jax
import jax.numpy as jnp
import numpy as np
from jax import lax

D = 6144
HEADS = 32
HEAD_DIM = 128
FF = 12288
NBR = 27
BRICK = 32
SECTIONS = 4
BRICKS = 24
TOKENS = 768
N_TENSOR = 16
N_SEQ = 8


def brick_tables(key):
    grid_side = 2
    while grid_side ** 3 < BRICKS:
        grid_side = grid_side + 1
    grid_cells = grid_side ** 3
    steps_range = np.arange(27)
    offsets = np.stack([steps_range // 9 - 1, steps_range // 3 % 3 - 1, steps_range % 3 - 1], 1).astype(np.int32)
    neighbour_list = []
    flag_list = []
    slot_list = []
    for section_index in range(SECTIONS):
        section_key = jax.random.fold_in(key, 7001 + section_index)
        cell_key, slot_key = jax.random.split(section_key)
        occupied = jax.random.permutation(cell_key, grid_cells)[:BRICKS].astype(jnp.int32)
        cell_owner = jnp.full((grid_cells,), -1, jnp.int32).at[occupied].set(jnp.arange(BRICKS, dtype=jnp.int32))
        coords = jnp.stack([occupied // (grid_side * grid_side), occupied // grid_side % grid_side, occupied % grid_side], 1)
        shifted = coords[:, None, :] + jnp.asarray(offsets)[None, :, :]
        inside = jnp.all((shifted >= 0) & (shifted < grid_side), axis=2)
        clipped = jnp.clip(shifted, 0, grid_side - 1)
        cell_index = clipped[:, :, 0] * grid_side * grid_side + clipped[:, :, 1] * grid_side + clipped[:, :, 2]
        found_brick = cell_owner[cell_index]
        is_valid = inside & (found_brick >= 0)
        own_brick = jnp.broadcast_to(jnp.arange(BRICKS, dtype=jnp.int32)[:, None], (BRICKS, 27))
        listed = jnp.where(is_valid, found_brick, own_brick).astype(jnp.int32)
        slot_of = jax.random.permutation(slot_key, BRICKS).astype(jnp.int32)
        holder = jnp.zeros((BRICKS,), jnp.int32).at[slot_of].set(jnp.arange(BRICKS, dtype=jnp.int32))
        neighbour_list.append(listed[holder])
        flag_list.append(is_valid[holder].astype(jnp.int32))
        slot_list.append(slot_of)
    return (jnp.stack(neighbour_list), jnp.stack(flag_list), jnp.stack(slot_list))


def draw_neighbours(key, part):
    return brick_tables(key)[0]


def draw_present(key, part):
    return brick_tables(key)[1]


def draw_brick_slot(key, part):
    return brick_tables(key)[2]


def draw_slot_bias(key, part):
    base_key = jax.random.fold_in(jax.random.fold_in(key, 3301), 0)
    values = jax.random.uniform(base_key, (SECTIONS, HEADS, NBR), jnp.float32, -3.0, 3.0)
    return values.astype(jnp.float32)


def steps_of(own_key, dims, shards, least, high):
    level = 1.0
    for dim, parts in shards:
        draws = jax.random.uniform(jax.random.fold_in(jax.random.fold_in(own_key, 6), dim), (parts,), jnp.float32, least / len(shards), high / len(shards))
        level = level * jnp.repeat(jnp.exp(draws), dims[dim] // parts).reshape((-1,) + (1,) * (len(dims) - 1 - dim))
    return level


def gaussian(stream_key, extent, deviation, most, cuts=(), held_as=jnp.bfloat16):
    factor_of = steps_of(stream_key, extent, cuts, -0.22, 0.18) if cuts else 1.0
    entries = jax.random.normal(stream_key, extent, jnp.float32) * deviation * factor_of
    return jnp.minimum(jnp.maximum(entries, -most), most).astype(held_as)


def setup_inputs(seed: int = 0) -> dict:
    keys = jax.random.split(jax.random.key(seed), 11)
    stream = gaussian(keys[0], (SECTIONS, TOKENS, D), 1.0, 6.0, ((0, 4), (1, 16), (2, 8)))
    norm_gain = jnp.clip(0.5 + 1.0 * jax.random.uniform(keys[1], (SECTIONS, D), jnp.float32) ** steps_of(keys[1], (SECTIONS, D), ((0, 4), (1, 8)), -0.2, 0.2), 0.5, 1.5)
    qkv_weight = gaussian(keys[2], (SECTIONS, D, 3, HEADS * HEAD_DIM), D ** -0.5, 0.078125, ((0, 4), (1, 8), (3, 16)))
    up_weight = gaussian(keys[3], (SECTIONS, D, FF), D ** -0.5, 0.078125, ((0, 4), (1, 8), (2, 16)))
    out_weight = gaussian(keys[4], (SECTIONS, HEADS * HEAD_DIM, D), (4 * (HEADS * HEAD_DIM) ** -0.5), 0.375, ((0, 4), (1, 16), (2, 8)))
    down_weight = gaussian(keys[5], (SECTIONS, FF, D), FF ** -0.5, 0.0546875, ((0, 4), (1, 16), (2, 8)))
    slot_bias = draw_slot_bias(jax.random.fold_in(keys[10], 71), 0)
    neighbours = draw_neighbours(jax.random.fold_in(keys[10], 71), 0)
    present = draw_present(jax.random.fold_in(keys[10], 71), 0)
    brick_slot = draw_brick_slot(jax.random.fold_in(keys[10], 71), 0)
    return {"stream": stream, "norm_gain": norm_gain, "qkv_weight": qkv_weight, "up_weight": up_weight, "out_weight": out_weight, "down_weight": down_weight, "slot_bias": slot_bias, "neighbours": neighbours, "present": present, "brick_slot": brick_slot}


def rounded(value):
    return lax.optimization_barrier(value.astype(jnp.bfloat16)).astype(jnp.float32)

def normalize(stream_rows, gain_row):
    values = stream_rows.astype(jnp.float32)
    center = lax.optimization_barrier(jnp.mean(values, axis=1, keepdims=True))
    second = lax.optimization_barrier(jnp.mean(values * values, axis=1, keepdims=True))
    spread = second - center * center
    return ((values - center) * lax.rsqrt(spread + 1e-06) * gain_row[None, :]).astype(jnp.bfloat16)

def brick_attention(key_bricks, value_bricks, head_bias):
    score_scale = HEAD_DIM ** (-0.5)

    def one_brick(inputs):
        query_brick, key_slots, flag_row = inputs
        near_keys = key_bricks[key_slots].astype(jnp.float32)
        near_values = value_bricks[key_slots].astype(jnp.float32)
        scores = jnp.einsum('qhd,jkhd->hqjk', query_brick.astype(jnp.float32), near_keys) * score_scale
        scores = scores + head_bias[:, None, :, None]
        usable = (flag_row > 0)[None, None, :, None]
        largest = lax.optimization_barrier(jnp.max(jnp.where(usable, scores, -1e+30), axis=(2, 3), keepdims=True))
        exp_scores = jnp.where(usable, jnp.exp(scores - largest), 0.0)
        totals = lax.optimization_barrier(jnp.sum(exp_scores, axis=(2, 3)))
        weights = rounded(exp_scores)
        mixed_sum = jnp.einsum('hqjk,jkhd->qhd', weights, near_values)
        return (mixed_sum / jnp.transpose(totals)[:, :, None]).astype(jnp.bfloat16)
    return one_brick

def section_layer(stream_rows, gain_row, qkv_part, up_part, out_part, down_part, head_bias, neighbour_rows, flag_rows, slot_row):
    normed = normalize(stream_rows, gain_row)
    head_width = HEADS * HEAD_DIM
    qkv_flat = qkv_part.reshape(D, 3 * head_width)
    block_rows = D // N_SEQ
    qkv_sum = jnp.zeros((TOKENS, 3 * head_width), jnp.float32)
    up_sum = jnp.zeros((TOKENS, FF), jnp.float32)
    for block_index in range(N_SEQ):
        lower = block_index * block_rows
        upper = lower + block_rows
        qkv_sum = qkv_sum + rounded(jnp.dot(normed[:, lower:upper], qkv_flat[lower:upper], preferred_element_type=jnp.float32))
        up_sum = up_sum + rounded(jnp.dot(normed[:, lower:upper], up_part[lower:upper], preferred_element_type=jnp.float32))
    qkv_rows = qkv_sum.astype(jnp.bfloat16)
    hidden = jax.nn.gelu(up_sum, approximate=False).astype(jnp.bfloat16)
    query_bricks = qkv_rows[:, :head_width].reshape(BRICKS, BRICK, HEADS, HEAD_DIM)
    key_bricks = qkv_rows[:, head_width:2 * head_width].reshape(BRICKS, BRICK, HEADS, HEAD_DIM)
    value_bricks = qkv_rows[:, 2 * head_width:].reshape(BRICKS, BRICK, HEADS, HEAD_DIM)
    key_slots = slot_row[neighbour_rows].astype(jnp.int32)
    attended = lax.map(brick_attention(key_bricks, value_bricks, head_bias), (query_bricks, key_slots, flag_rows))
    attended = attended.reshape(TOKENS, head_width)
    head_block = head_width // N_TENSOR
    hidden_block = FF // N_TENSOR
    update = jnp.zeros((TOKENS, D), jnp.float32)
    for block_index in range(N_TENSOR):
        head_low = block_index * head_block
        hidden_low = block_index * hidden_block
        term = jnp.dot(attended[:, head_low:head_low + head_block], out_part[head_low:head_low + head_block], preferred_element_type=jnp.float32)
        term = term + jnp.dot(hidden[:, hidden_low:hidden_low + hidden_block], down_part[hidden_low:hidden_low + hidden_block], preferred_element_type=jnp.float32)
        update = update + rounded(term)
    return (stream_rows.astype(jnp.float32) + update).astype(jnp.bfloat16)

def reference(stream, norm_gain, qkv_weight, up_weight, out_weight, down_weight, slot_bias, neighbours, present, brick_slot):
    results = []
    for section_index in range(SECTIONS):
        results.append(section_layer(stream[section_index], norm_gain[section_index], qkv_weight[section_index], up_weight[section_index], out_weight[section_index], down_weight[section_index], slot_bias[section_index], neighbours[section_index], present[section_index], brick_slot[section_index]))
    return jnp.roll(jnp.stack(results), 1, axis=0)
```

```python
import functools
import math

import jax
import jax.numpy as jnp
from jax import lax
from jax.experimental import pallas as pl
from jax.experimental.pallas import tpu as pltpu
from jax.sharding import PartitionSpec as P

HD = 128
BRICK = 32
NBR = 27
RINGZ = 8
CHIPS = 4
MESH = pl.DeviceIdType.MESH
F32 = jnp.float32
BF16 = jnp.bfloat16


def _dot(a, b):
    return jnp.dot(a, b, preferred_element_type=F32)


def kernel(
    dims,
    x_in, gain_in, qkv_in, up_in, out_in, down_in, nb_in, pr_in, bs_in, sb_ref,
    o_ref,
    xv, gain, w1q, w1u, w2, nbv, prv, bsv,
    st_t, st_snd, st_rcv, tab, bias,
    xg,
    psq, psu, rsq, rsu, poq, pou, soq, sou, roq, rou, nsq, nsu, rnq, rnu,
    qb, kvb, jb,
    fown, es3, es, er, lsnd, lrcv, res,
    sem_loc, sem_st, sem_tab, sem_a, sem_sib, sem_o, sem_n, sem_kv, sem_d, sem_df, sem_e, sem_l, sem_sec,
):
    RB, FD, UC, CO, BPD, DW, SECT = dims
    AH = HD + UC
    PB = CHIPS * RB
    sect = lax.axis_index("section")
    tens = lax.axis_index("tensor")
    seq = lax.axis_index("seq")
    z, l = lax.div(tens, 2), lax.rem(tens, 2)
    i, c = lax.div(seq, 2), lax.rem(seq, 2)
    zp = {"tensor": lax.rem(z + 1, RINGZ) * 2 + l}
    zm = {"tensor": lax.rem(z + RINGZ - 1, RINGZ) * 2 + l}
    lp = {"tensor": z * 2 + 1 - l}
    ip = lax.rem(i + 1, CHIPS)
    im = lax.rem(i + 3, CHIPS)
    io = lax.rem(i + 2, CHIPS)
    dp = {"seq": ip * 2 + c}
    dm = {"seq": im * 2 + c}
    sib = {"seq": i * 2 + 1 - c}
    sec_next = {"section": lax.rem(sect + 1, SECT)}
    sec_prev = {"section": lax.rem(sect + SECT - 1, SECT)}

    sends = []

    def rcopy(src, dst, sem, dev):
        return pltpu.make_async_remote_copy(
            src_ref=src, dst_ref=dst, send_sem=sem.at[0], recv_sem=sem.at[1],
            device_id=dev, device_id_type=MESH,
        )

    def send(src, dst, sem, dev):
        d = rcopy(src, dst, sem, dev)
        d.start()
        sends.append(d)

    def recv(dst, sem, dev):
        rcopy(dst, dst, sem, dev).wait_recv()

    loads = []

    def load(src, dst):
        d = pltpu.make_async_copy(src, dst, sem_loc.at[len(loads)])
        d.start()
        loads.append(d)
        return d

    ld_x = load(x_in, xv)
    ld_g = load(gain_in, gain)
    ld_t = [load(nb_in, nbv), load(pr_in, prv), load(bs_in, bsv)]
    ld_w = []
    for hf in range(2):
        cc = c if hf == 0 else 1 - c
        hcol = pl.ds(pl.multiple_of(cc * HD, HD), HD)
        ucol = pl.ds(pl.multiple_of(cc * UC, HD), UC)
        for g in range(3):
            ld_w.append(load(qkv_in.at[g, :, hcol], w1q.at[hf, :, g * HD : (g + 1) * HD]))
        ld_w.append(load(up_in.at[:, ucol], w1u.at[hf]))
    ld_w2 = []
    for hf in range(2):
        cc = c if hf == 0 else 1 - c
        ld_w2.append(load(out_in.at[pl.ds(pl.multiple_of(cc * HD, HD), HD), :], w2.at[hf, 0:HD]))
        ld_w2.append(load(down_in.at[pl.ds(pl.multiple_of(cc * UC, HD), UC), :], w2.at[hf, HD:AH]))

    barrier = pltpu.get_barrier_semaphore()
    peers = []
    for k in range(1, 8):
        peers.append({"seq": lax.rem(seq + k, 8)})
    greet = peers + [zp, zm, lp] + ([sec_prev] if SECT > 1 else [])
    for dev in greet:
        pl.semaphore_signal(barrier, inc=1, device_id=dev, device_id_type=MESH)

    ld_x.wait()
    xf = xv[...].astype(F32)
    s1 = jnp.sum(xf, axis=1, keepdims=True)
    s2 = jnp.sum(xf * xf, axis=1, keepdims=True)
    lane = lax.broadcasted_iota(jnp.int32, (RB, 128), 1)
    st_t[...] = jnp.zeros((128, 128), F32)
    st_t[0:RB, :] = jnp.where(lane == 0, s1, jnp.where(lane == 1, s2, 0.0))
    st_snd[...] = st_t[...].T[0:8, :]
    for d in ld_t:
        d.wait()
    tab[0] = jnp.full((8, 128), -1, jnp.int32)
    for q in range(BPD):
        tab[0, q : q + 1, 0:NBR] = jnp.where(prv[q] > 0, nbv[q], -1)
    pl.semaphore_wait(barrier, len(greet))
    for k in range(1, 8):
        send(st_snd, st_rcv.at[k - 1], sem_st.at[k - 1], peers[k - 1])
    for k in range(1, 8):
        send(tab.at[0], tab.at[k], sem_tab.at[k - 1], peers[k - 1])
    tot = st_snd[...]
    for k in range(1, 8):
        recv(st_rcv.at[k - 1], sem_st.at[k - 1], peers[k - 1])
        tot = tot + st_rcv[k - 1]
    st_t[0:8, :] = tot * (1.0 / DW)
    cols = st_t[...].T
    mean = cols[0:RB, 0:1]
    sq = cols[0:RB, 1:2]
    ld_g.wait()
    normed = (xf - mean) * lax.rsqrt(sq - mean * mean + 1e-06) * gain[...]
    xg[0, 0:RB] = normed.astype(BF16)

    def slot(m, sgn, lr):
        lo = RB * (2 * sgn + lr)
        return xg.at[m, lo : lo + RB]

    def a_sem(m, sgn, lr):
        return sem_a.at[m * 4 + sgn * 2 + lr]

    def a_send(src, dst, dev):
        send(slot(*src), slot(*dst), a_sem(*dst), dev)

    def a_recv(*dst):
        recv(slot(*dst), a_sem(*dst), zp)

    a_send((0, 0, 0), (0, 0, 1), lp)
    a_send((0, 0, 0), (1, 1, 0), zp)
    a_send((0, 0, 0), (1, 0, 0), zm)
    a_recv(0, 0, 1)
    a_send((0, 0, 1), (1, 1, 1), zp)
    a_send((0, 0, 1), (1, 0, 1), zm)

    def token_of(m, j, row):
        sgn, lr = lax.shift_right_logical(j, 1), lax.bitwise_and(j, 1)
        zo = jnp.where(m == 0, 4 * sgn, jnp.where(sgn == 0, m, RINGZ - m))
        zz = lax.bitwise_and(zo + z, RINGZ - 1)
        ll = lax.bitwise_and(lr + l, 1)
        return (2 * zz + ll) * RB + row

    def blocks(k):
        b = lax.shift_right_logical(k * (65536 // RB + 1), 16)
        return b, k - b * RB

    KEYS = 4 * PB
    QROWS = 4 * RB
    for k in range(1, 8):
        recv(tab.at[k], sem_tab.at[k - 1], peers[k - 1])
    enc = tab[...].reshape(64, 128)
    brick_id = lax.broadcasted_iota(jnp.int32, (64, 128), 1)
    near = jnp.full((64, 128), -1e30, F32)
    for j in range(NBR):
        near = jnp.where(enc[:, j : j + 1] == brick_id, sb_ref[c, j], near)
    key_i = lax.broadcasted_iota(jnp.int32, (1, KEYS), 1)
    kb, krow = blocks(key_i)
    kslot = lax.shift_right_logical(
        token_of(lax.shift_right_logical(kb, 2), lax.bitwise_and(kb, 3), krow), 5
    )
    eye = lax.broadcasted_iota(jnp.int32, (128, 128), 0) == lax.broadcasted_iota(
        jnp.int32, (128, 128), 1
    )
    bs_row = jnp.pad(bsv[...], ((0, 0), (0, 128 - 8 * BPD)), constant_values=-1).astype(F32)
    bs_col = jnp.sum(jnp.where(eye, bs_row, 0.0), axis=1, keepdims=True).astype(jnp.int32)
    of_key = jnp.where(bs_col == kslot, 1.0, 0.0)
    near_keys = jnp.dot(near, of_key, precision=lax.Precision.HIGHEST, preferred_element_type=F32)
    q_i = lax.broadcasted_iota(jnp.int32, (QROWS, 1), 0)
    qm, qrow = blocks(q_i)
    qslot = lax.shift_right_logical(token_of(qm, i + jnp.zeros_like(qm), qrow), 5)
    qdev = lax.shift_right_logical(qslot * (512 // BPD + 1), 9)
    qpos = 8 * lax.bitwise_and(seq + 8 - qdev, 7) + (qslot - BPD * qdev)
    of_query = jnp.where(qpos == lax.broadcasted_iota(jnp.int32, (1, 64), 1), 1.0, 0.0)
    bias[...] = jnp.dot(
        of_query, near_keys, precision=lax.Precision.HIGHEST, preferred_element_type=F32
    )

    ps, rs, po = (psq, psu), (rsq, rsu), (poq, pou)
    so, ro, ns, rn = (soq, sou), (roq, rou), (nsq, nsu), (rnq, rnu)
    w1 = (w1q, w1u)

    def rows(j):
        return pl.ds(pl.multiple_of(j * RB, 16), RB)

    def gather_stage(m):
        if m == 0:
            a_recv(0, 1, 0)
            a_recv(0, 1, 1)
            return
        for lr in range(2):
            for sgn in range(2):
                a_recv(m, sgn, lr)
                dev = zp if sgn == 1 else zm
                if m < 3:
                    a_send((m, sgn, lr), (m + 1, sgn, lr), dev)
                elif lr == sgn:
                    a_send((3, sgn, lr), (0, 1, lr), dev)

    def project(p, m):
        ps[p][m] = _dot(xg[m], w1[p][1]).astype(BF16)
        send(ps[p].at[m], rs[p].at[m], sem_sib.at[p, m], sib)
        po[p][m] = _dot(xg[m], w1[p][0])
        recv(rs[p].at[m], sem_sib.at[p, m], sib)
        so[p][m] = (po[p][m, rows(io), :] + rs[p][m, rows(io), :].astype(F32)).astype(BF16)
        send(so[p].at[m], ro[p].at[m], sem_o.at[p, m], dp if m % 2 == 0 else dm)

    def relay(p, m):
        recv(ro[p].at[m], sem_o.at[p, m], dp)
        for d, (j, dev) in enumerate(((ip, dp), (im, dm))):
            v = po[p][m, rows(j), :] + rs[p][m, rows(j), :].astype(F32)
            if d == m % 2:
                v = v + ro[p][m].astype(F32)
            ns[p][d, m] = v.astype(BF16)
            send(ns[p].at[d, m], rn[p].at[d, m], sem_n.at[p, d, m], dev)

    def reduced(p, m):
        v = po[p][m, rows(i), :] + rs[p][m, rows(i), :].astype(F32)
        for d in range(2):
            recv(rn[p].at[d, m], sem_n.at[p, d, m], dp)
            v = v + rn[p][d, m].astype(F32)
        return v

    def kv_rows(m, j):
        return kvb.at[pl.ds(pl.multiple_of(m * PB + j * RB, 16), RB)]

    def finish_qkv(m):
        v = reduced(0, m).astype(BF16)
        qb[m] = v[:, 0:HD]
        own = kv_rows(m, i)
        own[...] = v[:, HD:]
        send(own, own, sem_kv.at[m, 0], dp)
        send(own, own, sem_kv.at[m, 1], dm)

    def kv_relay(m):
        recv(kv_rows(m, im), sem_kv.at[m, 0], dp)
        recv(kv_rows(m, ip), sem_kv.at[m, 1], dp)
        j, dev = (im, dp) if m % 2 == 0 else (ip, dm)
        send(kv_rows(m, j), kv_rows(m, j), sem_kv.at[m, 2], dev)

    span = ((0, HD), (HD, AH))

    def j_part(hf, part, m, j):
        return jb.at[hf, m, rows(j), span[part][0] : span[part][1]]

    def spread(part, m):
        own = j_part(0, part, m, i)
        send(own, own, sem_d.at[part, m, 0], dp)
        send(own, own, sem_d.at[part, m, 1], dm)
        send(own, j_part(1, part, m, i), sem_df.at[part, m, 0], sib)

    def spread_relay(part, m):
        for d, j in enumerate((im, ip)):
            got = j_part(0, part, m, j)
            recv(got, sem_d.at[part, m, d], dp)
            if d == m % 2:
                send(got, got, sem_d.at[part, m, 2], dp if d == 0 else dm)
            send(got, j_part(1, part, m, j), sem_df.at[part, m, 1 + d], sib)

    def spread_last(part, m):
        got = j_part(0, part, m, io)
        recv(got, sem_d.at[part, m, 2], dp)
        send(got, j_part(1, part, m, io), sem_df.at[part, m, 3], sib)

    def spread_sib(part, m):
        for k, j in enumerate((i, im, ip, io)):
            recv(j_part(1, part, m, j), sem_df.at[part, m, k], sib)

    def finish_up(m):
        u = reduced(1, m)
        h = u * (1.0 + lax.erf(u * (1.0 / math.sqrt(2.0)))) * 0.5
        jb[0, m, rows(i), HD:AH] = h.astype(BF16)
        spread(1, m)

    def attend():
        for m in range(4):
            recv(kv_rows(m, io), sem_kv.at[m, 2], dp)
        for m in range(4):
            s = lax.dot_general(
                qb[m], kvb[:, 0:HD], (((1,), (1,)), ((), ())), preferred_element_type=F32
            )
            s = s * (HD**-0.5) + bias[m * RB : (m + 1) * RB, :]
            e = jnp.exp(s - jnp.max(s, axis=1, keepdims=True))
            total = jnp.sum(e, axis=1, keepdims=True)
            a = _dot(e.astype(BF16), kvb[:, HD:]) / total
            jb[0, m, rows(i), 0:HD] = a.astype(BF16)
            spread(0, m)

    def contribute(m):
        for part in range(2):
            spread_last(part, m)
        f = _dot(jb[0, m], w2[0])
        for part in range(2):
            spread_sib(part, m)
        f = f + _dot(jb[1, m], w2[1])
        if m == 0:
            fown[...] = f[0 : 2 * RB]
            es3[...] = f[2 * RB :].astype(BF16)
            for lr, dev in ((0, zp), (1, zm)):
                blk = es3.at[lr * RB : (lr + 1) * RB]
                send(blk, er.at[3, lr, lr * RB : (lr + 1) * RB], sem_e.at[3, lr], dev)
            return
        for sgn, dev in ((0, zp), (1, zm)):
            v = f[2 * RB * sgn : 2 * RB * (sgn + 1)]
            if m == 3:
                lo = sgn * RB
                recv(er.at[3, sgn, lo : lo + RB], sem_e.at[3, sgn], dev)
                es[m - 1, sgn, lo : lo + RB] = (
                    v[lo : lo + RB] + er[3, sgn, lo : lo + RB].astype(F32)
                ).astype(BF16)
                no = RB - lo
                es[m - 1, sgn, no : no + RB] = v[no : no + RB].astype(BF16)
            else:
                recv(er.at[m, sgn], sem_e.at[m, sgn], dev)
                es[m - 1, sgn] = (v + er[m, sgn].astype(F32)).astype(BF16)
            send(es.at[m - 1, sgn], er.at[m - 1, sgn], sem_e.at[m - 1, sgn], dev)

    def last():
        for sgn in range(2):
            recv(er.at[0, sgn], sem_e.at[0, sgn], zp)
        v = fown[...] + er[0, 0].astype(F32) + er[0, 1].astype(F32)
        lsnd[...] = v[RB:].astype(BF16)
        send(lsnd, lrcv, sem_l, lp)
        base = xv[...].astype(F32) + v[0:RB]
        recv(lrcv, sem_l, lp)
        res[...] = (base + lrcv[...].astype(F32)).astype(BF16)
        if SECT > 1:
            send(res, o_ref, sem_sec, sec_next)
        else:
            d = pltpu.make_async_copy(res, o_ref, sem_loc.at[0])
            d.start()
            d.wait()

    gather_stage(1)
    for d in ld_w:
        d.wait()
    project(0, 1)
    gather_stage(2)
    project(0, 2)
    relay(0, 1)
    gather_stage(3)
    project(0, 3)
    relay(0, 2)
    finish_qkv(1)
    gather_stage(0)
    project(0, 0)
    relay(0, 3)
    finish_qkv(2)
    project(1, 0)
    relay(0, 0)
    finish_qkv(3)
    kv_relay(1)
    project(1, 3)
    relay(1, 0)
    finish_qkv(0)
    kv_relay(2)
    project(1, 2)
    relay(1, 3)
    kv_relay(3)
    finish_up(0)
    project(1, 1)
    kv_relay(0)
    relay(1, 2)
    finish_up(3)
    attend()
    relay(1, 1)
    spread_relay(1, 0)
    finish_up(2)
    for m in (0, 3, 2, 1):
        spread_relay(0, m)
    spread_relay(1, 3)
    finish_up(1)
    for d in ld_w2:
        d.wait()
    contribute(0)
    spread_relay(1, 2)
    contribute(3)
    spread_relay(1, 1)
    contribute(2)
    contribute(1)
    last()
    for d in sends:
        d.wait_send()
    if SECT > 1:
        recv(o_ref, sem_sec, sec_next)


def per_device(sect, x, gain, qkv, up, out, down, sb, nb, pr, bs):
    RB, FD = x.shape[1:]
    UC = up.shape[2] // 2
    CO = out.shape[2]
    BPD = nb.shape[1]
    AH = HD + UC
    PB = CHIPS * RB
    QC = 3 * HD
    dims = (RB, FD, UC, CO, BPD, FD * 8, sect)
    vm, sm = pltpu.VMEM, pltpu.SemaphoreType.DMA
    scratch = [
        vm((RB, FD), BF16), vm((1, FD), F32), vm((2, FD, QC), BF16), vm((2, FD, UC), BF16),
        vm((2, AH, CO), BF16),
        vm((BPD, 1, NBR), jnp.int32), vm((BPD, 1, NBR), jnp.int32), vm((1, 8 * BPD), jnp.int32),
        vm((128, 128), F32), vm((8, 128), F32), vm((7, 8, 128), F32), vm((8, 8, 128), jnp.int32),
        vm((4 * RB, 4 * PB), F32),
        vm((4, PB, FD), BF16),
    ]
    two = (QC, UC)
    scratch += [vm((4, PB, w), BF16) for w in two]
    scratch += [vm((4, PB, w), BF16) for w in two]
    scratch += [vm((4, PB, w), F32) for w in two]
    scratch += [vm((4, RB, w), BF16) for w in two]
    scratch += [vm((4, RB, w), BF16) for w in two]
    scratch += [vm((2, 4, RB, w), BF16) for w in two]
    scratch += [vm((2, 4, RB, w), BF16) for w in two]
    scratch += [
        vm((4, RB, HD), BF16), vm((4 * PB, 2 * HD), BF16), vm((2, 4, PB, AH), BF16),
        vm((2 * RB, CO), F32), vm((2 * RB, CO), BF16), vm((3, 2, 2 * RB, CO), BF16),
        vm((4, 2, 2 * RB, CO), BF16), vm((RB, CO), BF16), vm((RB, CO), BF16), vm((RB, CO), BF16),
        sm((20,)), sm((7, 2)), sm((7, 2)), sm((16, 2)), sm((2, 4, 2)), sm((2, 4, 2)),
        sm((2, 2, 4, 2)), sm((4, 3, 2)), sm((2, 4, 3, 2)), sm((2, 4, 4, 2)), sm((4, 2, 2)),
        sm((2,)), sm((2,)),
    ]
    hbm = pl.BlockSpec(memory_space=pl.ANY)
    y = pl.pallas_call(
        functools.partial(kernel, dims),
        out_shape=jax.ShapeDtypeStruct((RB, CO), BF16),
        in_specs=[hbm] * 9 + [pl.BlockSpec(memory_space=pltpu.SMEM)],
        out_specs=hbm,
        scratch_shapes=scratch,
        compiler_params=pltpu.CompilerParams(
            collective_id=0, has_side_effects=True, vmem_limit_bytes=56 * 2**20
        ),
    )(
        x[0], gain, jnp.transpose(qkv[0], (1, 0, 2)), up[0], out[0], down[0],
        jnp.transpose(nb, (1, 0, 2)), jnp.transpose(pr, (1, 0, 2)), bs, sb[0],
    )
    return y[None]


def solution(mesh):
    return jax.shard_map(
        functools.partial(per_device, mesh.shape["section"]),
        mesh=mesh,
        in_specs=(
            P("section", "tensor", "seq"),
            P("section", "seq"),
            P("section", "seq", None, "tensor"),
            P("section", "seq", "tensor"),
            P("section", "tensor", "seq"),
            P("section", "tensor", "seq"),
            P("section", "tensor", None),
            P("section", "seq", None),
            P("section", "seq", None),
            P("section", None),
        ),
        out_specs=P("section", "tensor", "seq"),
        check_vma=False,
    )
```

```python
import functools
import math

import jax
import jax.numpy as jnp
from jax import lax
from jax.experimental import pallas as pl
from jax.experimental.pallas import tpu as pltpu
from jax.sharding import PartitionSpec as P

HD = 128
BRICK = 32
NBR = 27
RINGZ = 8
CHIPS = 4
MESH = pl.DeviceIdType.MESH
F32 = jnp.float32
BF16 = jnp.bfloat16


def _dot(a, b):
    return jnp.dot(a, b, preferred_element_type=F32)


def kernel(
    dims,
    x_in, gain_in, qkv_in, up_in, out_in, down_in, nb_in, pr_in, bs_in, sb_ref,
    o_ref,
    xv, gain, w1q, w1u, w2, nbv, prv, bsv,
    st_t, st_grp, st_own, st_all, bias,
    xg, gvs, gvg, gm, xc,
    psq, psu, rsq, rsu, poq, pou, sou, rou, nsq, nsu, rnq, rnu,
    qb, kvb, jb,
    fown, fbuf, es3, es, er, fin, lsnd, lrcv, res,
    sem_loc, sem_st, sem_g, sem_all, sem_a, sem_sib, sem_o, sem_n, sem_kv, sem_d, sem_df, sem_e, sem_f, sem_l, sem_sec,
):
    RB, FD, UC, CO, BPD, DW, SECT = dims
    AH = HD + UC
    PB = CHIPS * RB
    sect = lax.axis_index("section")
    tens = lax.axis_index("tensor")
    seq = lax.axis_index("seq")
    z, l = lax.div(tens, 2), lax.rem(tens, 2)
    i, c = lax.div(seq, 2), lax.rem(seq, 2)
    zp = {"tensor": lax.rem(z + 1, RINGZ) * 2 + l}
    zm = {"tensor": lax.rem(z + RINGZ - 1, RINGZ) * 2 + l}
    zpo = {"tensor": lax.rem(z + 1, RINGZ) * 2 + 1 - l}
    zmo = {"tensor": lax.rem(z + RINGZ - 1, RINGZ) * 2 + 1 - l}
    lp = {"tensor": z * 2 + 1 - l}
    ip = lax.rem(i + 1, CHIPS)
    im = lax.rem(i + 3, CHIPS)
    io = lax.rem(i + 2, CHIPS)
    dp = {"seq": ip * 2 + c}
    dm = {"seq": im * 2 + c}
    do = {"seq": io * 2 + c}
    sib = {"seq": i * 2 + 1 - c}
    sec_next = {"section": lax.rem(sect + 1, SECT)}
    sec_prev = {"section": lax.rem(sect + SECT - 1, SECT)}

    sends = []

    def rcopy(src, dst, sem, dev):
        return pltpu.make_async_remote_copy(
            src_ref=src, dst_ref=dst, send_sem=sem.at[0], recv_sem=sem.at[1],
            device_id=dev, device_id_type=MESH,
        )

    def send(src, dst, sem, dev):
        d = rcopy(src, dst, sem, dev)
        d.start()
        sends.append(d)

    def recv(dst, sem, dev):
        rcopy(dst, dst, sem, dev).wait_recv()

    loads = []

    def load(src, dst):
        d = pltpu.make_async_copy(src, dst, sem_loc.at[len(loads)])
        d.start()
        loads.append(d)
        return d

    ld_x = load(x_in, xv)
    ld_g = load(gain_in, gain)
    ld_t = [load(nb_in, nbv), load(pr_in, prv), load(bs_in, bsv)]
    ld_w = []
    for hf in range(2):
        cc = c if hf == 0 else 1 - c
        hcol = pl.ds(pl.multiple_of(cc * HD, HD), HD)
        ucol = pl.ds(pl.multiple_of(cc * UC, HD), UC)
        for g in range(3):
            ld_w.append(load(qkv_in.at[g, :, hcol], w1q.at[hf, :, g * HD : (g + 1) * HD]))
        ld_w.append(load(up_in.at[:, ucol], w1u.at[hf]))
    ld_w2 = []
    for hf in range(2):
        cc = c if hf == 0 else 1 - c
        ld_w2.append(load(out_in.at[pl.ds(pl.multiple_of(cc * HD, HD), HD), :], w2.at[hf, 0:HD]))
        ld_w2.append(load(down_in.at[pl.ds(pl.multiple_of(cc * UC, HD), UC), :], w2.at[hf, HD:AH]))

    barrier = pltpu.get_barrier_semaphore()
    peers = [{"seq": lax.rem(seq + k, 8)} for k in range(1, 8)]
    kin = []
    for dz in range(RINGZ):
        for lr in range(2):
            if dz + lr:
                zz = lax.rem(z + dz, RINGZ)
                dev = {"tensor": zz * 2 + (l if lr == 0 else 1 - l)}
                place = (0, 1) if dz == 4 else (dz, 1) if dz < 4 else (RINGZ - dz, 0)
                kin.append((dev, place + (lr,) if dz else (0, 0, lr)))
    greet = peers + [dev for dev, _ in kin] + ([sec_prev] if SECT > 1 else [])
    for dev in greet:
        pl.semaphore_signal(barrier, inc=1, device_id=dev, device_id_type=MESH)

    ld_x.wait()
    ld_g.wait()
    xf = xv[...].astype(F32)
    s1 = jnp.sum(xf, axis=1, keepdims=True)
    s2 = jnp.sum(xf * xf, axis=1, keepdims=True)
    xc[...] = ((xf - s1 * (1.0 / FD)) * gain[...]).astype(BF16)
    lane = lax.broadcasted_iota(jnp.int32, (RB, 128), 1)
    st_t[...] = jnp.zeros((128, 128), F32)
    st_t[0:RB, :] = jnp.where(lane == 0, s1, jnp.where(lane == 1, s2, 0.0))
    st_grp[0] = st_t[...].T[0:8, :]
    for d in ld_t:
        d.wait()
    st_grp[0, 2:8] = jnp.full((6, 128), -1.0, F32)
    for q in range(BPD):
        st_grp[0, 2 + q : 3 + q, 0:NBR] = jnp.where(prv[q] > 0, nbv[q], -1).astype(F32)
    for d in ld_w:
        d.wait()
    g1 = gain[...].astype(BF16).astype(F32)
    g2 = (gain[...] - g1).astype(BF16).astype(F32)
    g3 = gain[...] - g1 - g2
    part_i = lax.broadcasted_iota(jnp.int32, (8, FD), 0)
    parts = jnp.where(part_i == 0, g1, jnp.where(part_i == 1, g2, jnp.where(part_i == 2, g3, 0.0)))
    parts = parts.astype(BF16)
    QC = 3 * HD
    for hf in range(2):
        gvs[hf, :, 0:QC] = jnp.sum(_dot(parts, w1q[hf]), axis=0, keepdims=True)
        gvs[hf, :, QC : QC + UC] = jnp.sum(_dot(parts, w1u[hf]), axis=0, keepdims=True)
    gm[0:1, :] = gvs[0]
    pl.semaphore_wait(barrier, len(greet))

    def slot(m, sgn, lr):
        lo = RB * (2 * sgn + lr)
        return xg.at[m, lo : lo + RB]

    def a_sem(m, sgn, lr):
        return sem_a.at[m * 4 + sgn * 2 + lr]

    def a_send(src, dst, dev):
        send(slot(*src), slot(*dst), a_sem(*dst), dev)

    def a_recv(*dst):
        recv(slot(*dst), a_sem(*dst), zp)

    for dst, dev in (((0, 0, 1), lp), ((1, 1, 0), zp), ((1, 0, 0), zm)):
        send(xc, slot(*dst), a_sem(*dst), dev)
    for k in range(1, 8):
        send(st_grp.at[0], st_grp.at[k], sem_st.at[k - 1], peers[k - 1])
    for k in range(1, 8):
        send(gvs.at[k % 2], gvg.at[k - 1], sem_g.at[k - 1], peers[k - 1])
    xg[0, 0:RB] = xc[...]
    a_recv(0, 0, 1)
    a_send((0, 0, 1), (1, 1, 1), zp)
    a_send((0, 0, 1), (1, 0, 1), zm)
    for k in range(1, 8):
        recv(st_grp.at[k], sem_st.at[k - 1], peers[k - 1])
    tot = jnp.sum(st_grp[...], axis=0) * (1.0 / DW)
    mean = tot[0:1]
    for k in range(8):
        st_own[k : k + 1] = mean - st_grp[k, 0:1] * (1.0 / FD)
    st_own[8:16] = jnp.broadcast_to(lax.rsqrt(tot[1:2] - mean * mean + 1e-06), (8, 128))
    for dev, (m, sgn, lr) in kin:
        k = m * 4 + sgn * 2 + lr
        send(st_own, st_all.at[k], sem_all.at[k], dev)
    st_all[0] = st_own[...]

    def token_of(m, j, row):
        sgn, lr = lax.shift_right_logical(j, 1), lax.bitwise_and(j, 1)
        zo = jnp.where(m == 0, 4 * sgn, jnp.where(sgn == 0, m, RINGZ - m))
        zz = lax.bitwise_and(zo + z, RINGZ - 1)
        ll = lax.bitwise_and(lr + l, 1)
        return (2 * zz + ll) * RB + row

    def blocks(k):
        b = lax.shift_right_logical(k * (65536 // RB + 1), 16)
        return b, k - b * RB

    KEYS = 4 * PB
    QROWS = 4 * RB

    def make_bias():
        enc = st_grp[...].reshape(64, 128)
        brick_id = lax.broadcasted_iota(jnp.int32, (64, 128), 1).astype(F32)
        near = jnp.full((64, 128), -1e30, F32)
        for j in range(NBR):
            near = jnp.where(enc[:, j : j + 1] == brick_id, sb_ref[c, j], near)
        key_i = lax.broadcasted_iota(jnp.int32, (1, KEYS), 1)
        kb, krow = blocks(key_i)
        kslot = lax.shift_right_logical(
            token_of(lax.shift_right_logical(kb, 2), lax.bitwise_and(kb, 3), krow), 5
        )
        eye = lax.broadcasted_iota(jnp.int32, (128, 128), 0) == lax.broadcasted_iota(
            jnp.int32, (128, 128), 1
        )
        bs_row = jnp.pad(bsv[...], ((0, 0), (0, 128 - 8 * BPD)), constant_values=-1).astype(F32)
        bs_col = jnp.sum(jnp.where(eye, bs_row, 0.0), axis=1, keepdims=True).astype(jnp.int32)
        of_key = jnp.where(bs_col == kslot, 1.0, 0.0)
        near_keys = jnp.dot(near, of_key, precision=lax.Precision.HIGHEST, preferred_element_type=F32)
        q_i = lax.broadcasted_iota(jnp.int32, (QROWS, 1), 0)
        qm, qrow = blocks(q_i)
        qm = lax.bitwise_and(4 - qm, 3)
        qslot = lax.shift_right_logical(token_of(qm, i + jnp.zeros_like(qm), qrow), 5)
        qdev = lax.shift_right_logical(qslot * (512 // BPD + 1), 9)
        qpos = 8 * lax.bitwise_and(seq + 8 - qdev, 7) + 2 + (qslot - BPD * qdev)
        of_query = jnp.where(qpos == lax.broadcasted_iota(jnp.int32, (1, 64), 1), 1.0, 0.0)
        bias[...] = jnp.dot(
            of_query, near_keys, precision=lax.Precision.HIGHEST, preferred_element_type=F32
        )

    ps, rs, po = (psq, psu), (rsq, rsu), (poq, pou)
    so, ro, ns, rn = (None, sou), (None, rou), (nsq, nsu), (rnq, rnu)
    w1 = (w1q, w1u)

    def rows(j):
        return pl.ds(pl.multiple_of(j * RB, 16), RB)

    def gather_stage(m):
        if m == 0:
            a_recv(0, 1, 0)
            a_recv(0, 1, 1)
            return
        for lr in range(2):
            for sgn in range(2):
                a_recv(m, sgn, lr)
                dev = zp if sgn == 1 else zm
                if m < 3:
                    a_send((m, sgn, lr), (m + 1, sgn, lr), dev)
                elif lr == sgn:
                    a_send((3, sgn, lr), (0, 1, lr), dev)

    def take_sums():
        for _, (m, sgn, lr) in kin:
            k = m * 4 + sgn * 2 + lr
            recv(st_all.at[k], sem_all.at[k], zp)
        for k in range(1, 8):
            recv(gvg.at[k - 1], sem_g.at[k - 1], peers[k - 1])
            gm[k : k + 1, :] = gvg[k - 1]
        for m in range(4):
            st_t[16 * m : 16 * m + 16] = st_all[4 * m + i]
        st_t[...] = st_t[...].T

    def project(p, m):
        ps[p][m] = _dot(xg[m], w1[p][1]).astype(BF16)
        send(ps[p].at[m], rs[p].at[m], sem_sib.at[p, m], sib)
        po[p][m] = _dot(xg[m], w1[p][0])
        recv(rs[p].at[m], sem_sib.at[p, m], sib)
        if p == 0:
            for d, (j, dev) in enumerate(((ip, dp), (im, dm), (io, do))):
                v = po[p][m, rows(j), :] + rs[p][m, rows(j), :].astype(F32)
                nsq[d, m] = v.astype(BF16)
                send(nsq.at[d, m], rnq.at[d, m], sem_n.at[p, d, m], dev)
            return
        so[p][m] = (po[p][m, rows(io), :] + rs[p][m, rows(io), :].astype(F32)).astype(BF16)
        send(so[p].at[m], ro[p].at[m], sem_o.at[p, m], dp if m % 2 == 0 else dm)

    def relay(p, m):
        recv(ro[p].at[m], sem_o.at[p, m], dp)
        for d, (j, dev) in enumerate(((ip, dp), (im, dm))):
            v = po[p][m, rows(j), :] + rs[p][m, rows(j), :].astype(F32)
            if d == m % 2:
                v = v + ro[p][m].astype(F32)
            ns[p][d, m] = v.astype(BF16)
            send(ns[p].at[d, m], rn[p].at[d, m], sem_n.at[p, d, m], dev)

    def reduced(p, m):
        v = po[p][m, rows(i), :] + rs[p][m, rows(i), :].astype(F32)
        for d in range(2 if p else 3):
            recv(rn[p].at[d, m], sem_n.at[p, d, m], dp)
            v = v + rn[p][d, m].astype(F32)
        v = v - jnp.dot(
            st_t[0:RB, 16 * m : 16 * m + 8], gm[:, p * QC : p * QC + v.shape[1]],
            precision=lax.Precision.HIGHEST, preferred_element_type=F32,
        )
        return v * st_t[0:RB, 16 * m + 8 : 16 * m + 9]

    def kv_rows(m, j):
        return kvb.at[pl.ds(pl.multiple_of(m * PB + j * RB, 16), RB)]

    def finish_qkv(m):
        v = reduced(0, m).astype(BF16)
        at = (4 - m) % 4 * RB
        qb[at : at + RB] = v[:, 0:HD]
        own = kv_rows(m, i)
        own[...] = v[:, HD:]
        send(own, own, sem_kv.at[m, 0], dp)
        send(own, own, sem_kv.at[m, 1], dm)
        send(own, own, sem_kv.at[m, 2], do)

    span = ((0, HD), (HD, AH))

    def j_part(hf, part, m, j):
        return jb.at[hf, m, rows(j), span[part][0] : span[part][1]]

    def spread(part, m):
        own = j_part(0, part, m, i)
        send(own, own, sem_d.at[part, m, 0], dp)
        send(own, own, sem_d.at[part, m, 1], dm)
        send(own, j_part(1, part, m, i), sem_df.at[part, m, 0], sib)

    def spread_relay(part, m):
        for d, j in enumerate((im, ip)):
            got = j_part(0, part, m, j)
            recv(got, sem_d.at[part, m, d], dp)
            if d == m % 2:
                send(got, got, sem_d.at[part, m, 2], dp if d == 0 else dm)
            send(got, j_part(1, part, m, j), sem_df.at[part, m, 1 + d], sib)

    def spread_last(part, m):
        got = j_part(0, part, m, io)
        recv(got, sem_d.at[part, m, 2], dp)
        send(got, j_part(1, part, m, io), sem_df.at[part, m, 3], sib)

    def spread_sib(part, m):
        for k, j in enumerate((i, im, ip, io)):
            recv(j_part(1, part, m, j), sem_df.at[part, m, k], sib)

    def finish_up(m):
        u = reduced(1, m)
        h = u * (1.0 + lax.erf(u * (1.0 / math.sqrt(2.0)))) * 0.5
        jb[0, m, rows(i), HD:AH] = h.astype(BF16)
        spread(1, m)

    def attend():
        for m in range(4):
            for d, j in enumerate((im, ip, io)):
                recv(kv_rows(m, j), sem_kv.at[m, d], dp)
        for two in ((0, 3), (2, 1)):
            lo = (4 - two[0]) % 4 * RB
            s = lax.dot_general(
                qb[lo : lo + 2 * RB], kvb[:, 0:HD], (((1,), (1,)), ((), ())),
                preferred_element_type=F32,
            )
            s = s * (HD**-0.5) + bias[lo : lo + 2 * RB, :]
            e = jnp.exp(s - jnp.max(s, axis=1, keepdims=True))
            total = jnp.sum(e, axis=1, keepdims=True)
            a = (_dot(e.astype(BF16), kvb[:, HD:]) / total).astype(BF16)
            for n, m in enumerate(two):
                jb[0, m, rows(i), 0:HD] = a[n * RB : (n + 1) * RB]
                spread(0, m)

    halves = [(h, slice(h * CO // 2, (h + 1) * CO // 2)) for h in range(2)]

    def contribute(m):
        for part in range(2):
            spread_last(part, m)
        fbuf[m] = _dot(jb[0, m], w2[0])
        for part in range(2):
            spread_sib(part, m)
        fbuf[m] += _dot(jb[1, m], w2[1])
        if m == 0:
            es3[...] = fbuf[0, 2 * RB :].astype(BF16)
            for h, cs in halves:
                for lr, dev in ((0, zp), (1, zm)):
                    blk = slice(lr * RB, (lr + 1) * RB)
                    send(es3.at[blk, cs], er.at[3, lr, blk, cs], sem_e.at[3, lr, h], dev)
            lsnd[...] = fbuf[0, RB : 2 * RB].astype(BF16)
            send(lsnd, lrcv, sem_l, lp)
            fown[...] = xv[...].astype(F32) + fbuf[0, 0:RB]
            return
        for h, cs in halves:
            for sgn, dev, far in ((0, zp, zpo), (1, zm, zmo)):
                lo = 2 * RB * sgn
                if m == 3:
                    a, b = sgn * RB, RB - sgn * RB
                    got = er.at[3, sgn, a : a + RB, cs]
                    recv(got, sem_e.at[3, sgn, h], dev)
                    es[2, sgn, a : a + RB, cs] = (
                        fbuf[3, lo + a : lo + a + RB, cs] + got[...].astype(F32)
                    ).astype(BF16)
                    es[2, sgn, b : b + RB, cs] = fbuf[3, lo + b : lo + b + RB, cs].astype(BF16)
                else:
                    got = er.at[m, sgn, :, cs]
                    recv(got, sem_e.at[m, sgn, h], dev)
                    es[m - 1, sgn, :, cs] = (
                        fbuf[m, lo : lo + 2 * RB, cs] + got[...].astype(F32)
                    ).astype(BF16)
                if m > 1:
                    send(
                        es.at[m - 1, sgn, :, cs], er.at[m - 1, sgn, :, cs],
                        sem_e.at[m - 1, sgn, h], dev,
                    )
                else:
                    for lr, to in ((1, far), (0, dev)):
                        send(
                            es.at[0, sgn, lr * RB : (lr + 1) * RB, cs],
                            fin.at[sgn, lr, :, cs], sem_f.at[sgn, lr, h], to,
                        )

    def last():
        recv(lrcv, sem_l, lp)
        for h, cs in halves:
            v = fown[:, cs] + lrcv[:, cs].astype(F32)
            for lr in range(2):
                for sgn in range(2):
                    recv(fin.at[sgn, lr, :, cs], sem_f.at[sgn, lr, h], zp)
                    v = v + fin[sgn, lr, :, cs].astype(F32)
            res[:, cs] = v.astype(BF16)
            if SECT > 1:
                send(res.at[:, cs], o_ref.at[:, cs], sem_sec.at[h], sec_next)
            else:
                d = pltpu.make_async_copy(res.at[:, cs], o_ref.at[:, cs], sem_loc.at[0])
                d.start()
                d.wait()

    gather_stage(1)
    project(0, 1)
    gather_stage(2)
    project(0, 2)
    make_bias()
    take_sums()
    gather_stage(3)
    project(0, 3)
    finish_qkv(1)
    gather_stage(0)
    project(0, 0)
    finish_qkv(2)
    project(1, 0)
    finish_qkv(3)
    project(1, 3)
    finish_qkv(0)
    relay(1, 0)
    project(1, 2)
    relay(1, 3)
    attend()
    finish_up(0)
    project(1, 1)
    relay(1, 2)
    finish_up(3)
    for d in ld_w2:
        d.wait()
    spread_relay(0, 0)
    spread_relay(0, 3)
    relay(1, 1)
    spread_relay(1, 0)
    finish_up(2)
    spread_relay(0, 2)
    spread_relay(0, 1)
    finish_up(1)
    spread_relay(1, 3)
    contribute(0)
    spread_relay(1, 2)
    contribute(3)
    spread_relay(1, 1)
    contribute(2)
    contribute(1)
    last()
    for d in sends:
        d.wait_send()
    if SECT > 1:
        for h, cs in halves:
            recv(o_ref.at[:, cs], sem_sec.at[h], sec_next)


def per_device(sect, x, gain, qkv, up, out, down, sb, nb, pr, bs):
    RB, FD = x.shape[1:]
    UC = up.shape[2] // 2
    CO = out.shape[2]
    BPD = nb.shape[1]
    AH = HD + UC
    PB = CHIPS * RB
    QC = 3 * HD
    dims = (RB, FD, UC, CO, BPD, FD * 8, sect)
    vm, sm = pltpu.VMEM, pltpu.SemaphoreType.DMA
    scratch = [
        vm((RB, FD), BF16), vm((1, FD), F32), vm((2, FD, QC), BF16), vm((2, FD, UC), BF16),
        vm((2, AH, CO), BF16),
        vm((BPD, 1, NBR), jnp.int32), vm((BPD, 1, NBR), jnp.int32), vm((1, 8 * BPD), jnp.int32),
        vm((128, 128), F32), vm((8, 8, 128), F32), vm((16, 128), F32), vm((16, 16, 128), F32),
        vm((4 * RB, 4 * PB), F32),
        vm((4, PB, FD), BF16), vm((2, 1, QC + UC), F32), vm((7, 1, QC + UC), F32), vm((8, QC + UC), F32),
        vm((RB, FD), BF16),
    ]
    two = (QC, UC)
    scratch += [vm((4, PB, w), BF16) for w in two]
    scratch += [vm((4, PB, w), BF16) for w in two]
    scratch += [vm((4, PB, w), F32) for w in two]
    scratch += [vm((4, RB, UC), BF16) for _ in range(2)]
    scratch += [vm((n, 4, RB, w), BF16) for n, w in ((3, QC), (2, UC))]
    scratch += [vm((n, 4, RB, w), BF16) for n, w in ((3, QC), (2, UC))]
    scratch += [
        vm((4 * RB, HD), BF16), vm((4 * PB, 2 * HD), BF16), vm((2, 4, PB, AH), BF16),
        vm((RB, CO), F32), vm((4, PB, CO), F32), vm((2 * RB, CO), BF16), vm((3, 2, 2 * RB, CO), BF16),
        vm((4, 2, 2 * RB, CO), BF16), vm((2, 2, RB, CO), BF16), vm((RB, CO), BF16), vm((RB, CO), BF16), vm((RB, CO), BF16),
        sm((20,)), sm((7, 2)), sm((7, 2)), sm((16, 2)), sm((16, 2)), sm((2, 4, 2)), sm((2, 4, 2)),
        sm((2, 3, 4, 2)), sm((4, 3, 2)), sm((2, 4, 3, 2)), sm((2, 4, 4, 2)), sm((4, 2, 2, 2)),
        sm((2, 2, 2, 2)), sm((2,)), sm((2, 2)),
    ]
    hbm = pl.BlockSpec(memory_space=pl.ANY)
    y = pl.pallas_call(
        functools.partial(kernel, dims),
        out_shape=jax.ShapeDtypeStruct((RB, CO), BF16),
        in_specs=[hbm] * 9 + [pl.BlockSpec(memory_space=pltpu.SMEM)],
        out_specs=hbm,
        scratch_shapes=scratch,
        compiler_params=pltpu.CompilerParams(
            collective_id=0, has_side_effects=True, vmem_limit_bytes=56 * 2**20
        ),
    )(
        x[0], gain, jnp.transpose(qkv[0], (1, 0, 2)), up[0], out[0], down[0],
        jnp.transpose(nb, (1, 0, 2)), jnp.transpose(pr, (1, 0, 2)), bs, sb[0],
    )
    return y[None]


def solution(mesh):
    return jax.shard_map(
        functools.partial(per_device, mesh.shape["section"]),
        mesh=mesh,
        in_specs=(
            P("section", "tensor", "seq"),
            P("section", "seq"),
            P("section", "seq", None, "tensor"),
            P("section", "seq", "tensor"),
            P("section", "tensor", "seq"),
            P("section", "tensor", "seq"),
            P("section", "tensor", None),
            P("section", "seq", None),
            P("section", "seq", None),
            P("section", None),
        ),
        out_specs=P("section", "tensor", "seq"),
        check_vma=False,
    )
```
